32 devices in a mesh: loop: 8 (over z, core), group: 4 (over y, x).
Axes of the slice: x: 2, y: 2, z: 4, core: 2. Of those that a mesh axis runs over, the one named last changes fastest.
Arguments:
- node_feats: bfloat16 [16384, 512], P(('loop', 'group')), may hold values from -64 to 64
- w_qkv: bfloat16 [512, 8, 192], P(None, 'group'), may hold values from -1 to 1
- w_out: bfloat16 [512, 512], P('group'), may hold values from -0.25 to 0.25
- tile_cols: int32 [128, 10], P('loop'), may hold values from 0 to 127, as said below
Outputs:
- attended: bfloat16 [16384, 512], P(('loop', 'group'))
The draws below stay inside these ranges and needn't reach their ends.
Inputs may be any that keep to these rules, and one draw needn't show every extreme that they name: `tile_cols`: each row names 10 distinct tiles, among them the row's own tile b; exactly 4 of them lie in the row's own node block of 16 tiles, and each of the others lies in a different other node block. Rows of one node block that name tiles of the same other node block name different tiles of it.
All inputs are finite; a program needn't handle non-finite values.
Results may differ from the reference program's by a relative error of at most 0.019.
Values may be sent and summed in bfloat16 or wider, within the bound.
A program may use at most 128 MiB of HBM per device.

```python
import jax
import jax.numpy as jnp
from jax import lax

D = 512
HEADS = 8
HD = 64
TILE = 128
K = 10
MOST = 4
TPS = 16
NODES = 16384
NBLOCKS = 128
N_LOOP = 8


def draw_tile_cols(key, part):
    key = jax.random.fold_in(key, 7)
    key_own, key_far, key_pick = jax.random.split(key, 3)
    rows = jnp.arange(NBLOCKS, dtype=jnp.int32)
    owner = rows // TPS
    own_pos = rows % TPS
    own_steps = jax.vmap(lambda sub: jax.random.permutation(sub, TPS - 1)[:MOST - 1] + 1)(jax.random.split(key_own, NBLOCKS))
    own_cols = owner[:, None] * TPS + (own_pos[:, None] + own_steps.astype(jnp.int32)) % TPS
    far_steps = jax.vmap(lambda sub: jax.random.permutation(sub, N_LOOP - 1)[:K - MOST] + 1)(jax.random.split(key_far, NBLOCKS))
    far_owner = (owner[:, None] + far_steps.astype(jnp.int32)) % N_LOOP
    offsets = jax.random.randint(key_pick, (N_LOOP, N_LOOP), 0, TPS).astype(jnp.int32)
    far_pos = (own_pos[:, None] + offsets[owner[:, None], far_owner]) % TPS
    far_cols = far_owner * TPS + far_pos
    return jnp.concatenate([rows[:, None], own_cols, far_cols], axis=1).astype(jnp.int32)


def draw_node_feats(key, part):
    key = jax.random.fold_in(key, 11)
    key_base = jax.random.fold_in(key, 0)
    base = jnp.clip(jax.random.normal(key_base, (NODES, D), jnp.float32), -4.0, 4.0)
    return base.astype(jnp.bfloat16)


def draw_w_qkv(key, part):
    key = jax.random.fold_in(key, 5)
    key_main = jax.random.fold_in(key, 0)
    raw = jax.random.normal(key_main, (D, HEADS, 3 * HD), jnp.float32) * D ** (-0.5)
    return raw.astype(jnp.bfloat16)


def levels(key, dims, shards, smallest, largest):
    def one(dim, shards_of):
        steps = jax.random.uniform(jax.random.fold_in(jax.random.fold_in(key, 6), dim), (shards_of,), jnp.float32, smallest / len(shards), largest / len(shards))
        return jnp.repeat(jnp.exp(steps), dims[dim] // shards_of).reshape((-1,) + (1,) * (len(dims) - dim - 1))

    loudness = one(*shards[0])
    for cut in shards[1:]:
        loudness = loudness * one(*cut)
    return loudness


def noise(own_key, dims, width, limit, cuts=(), kind=jnp.bfloat16):
    loudness = levels(own_key, dims, cuts, -0.22, 0.18) if cuts else 1.0
    values = jax.random.normal(own_key, dims, jnp.float32) * width * loudness
    return jnp.minimum(jnp.maximum(values, -limit), limit).astype(kind)


def setup_inputs(seed: int = 0) -> dict:
    splits = jax.random.split(jax.random.key(seed), 5)
    node_feats = draw_node_feats(jax.random.fold_in(splits[4], 71), 0)
    w_qkv = draw_w_qkv(jax.random.fold_in(splits[4], 71), 0)
    w_out = noise(splits[2], (HEADS * HD, D), (HEADS * HD) ** -0.5, 0.25, ((0, 4),))
    tile_cols = draw_tile_cols(jax.random.fold_in(splits[4], 71), 0)
    return {"node_feats": node_feats, "w_qkv": w_qkv, "w_out": w_out, "tile_cols": tile_cols}


def reference(node_feats, w_qkv, w_out, tile_cols):
    projected = jnp.einsum("nd,dhe->nhe", node_feats.astype(jnp.float32), w_qkv.astype(jnp.float32)).astype(jnp.bfloat16)
    nblock = NODES // TILE
    queries = projected[:, :, :HD].reshape(nblock, TILE, HEADS, HD)
    keyvals = projected[:, :, HD:].reshape(nblock, TILE, HEADS, 2 * HD)
    factor = 1.0 / (HD ** 0.5)

    def one_row(inputs):
        query_blk, columns = inputs
        kv_tiles = keyvals[columns].reshape(K * TILE, HEADS, 2 * HD)
        scores = jnp.einsum("qhe,jhe->hqj", query_blk.astype(jnp.float32), kv_tiles[:, :, :HD].astype(jnp.float32)) * factor
        top = jnp.max(scores, axis=-1, keepdims=True)
        weights = jnp.exp(scores - top)
        denom = jnp.sum(weights, axis=-1)
        summed = jnp.einsum("hqj,jhe->hqe", weights.astype(jnp.bfloat16).astype(jnp.float32), kv_tiles[:, :, HD:].astype(jnp.float32))
        mixed = (summed / denom[:, :, None]).astype(jnp.bfloat16)
        return jnp.transpose(mixed, (1, 0, 2)).reshape(TILE, HEADS * HD)

    mixed = lax.map(one_row, (queries, tile_cols)).reshape(NODES, HEADS * HD)
    return jnp.dot(mixed, w_out, preferred_element_type=jnp.float32).astype(jnp.bfloat16)
```

```python
import functools

import jax
import jax.numpy as jnp
from jax import lax
from jax.experimental import pallas as pl
from jax.experimental.pallas import tpu as pltpu
from jax.sharding import PartitionSpec as P

TILE = 128
LOG2E = 1.4426950408889634


def attend_kernel(heads, head_dim, cols_ref, q_ref, kv_ref, out_ref):
    row = pl.program_id(0)
    slots = cols_ref.shape[1]
    wide = 2 * head_dim
    factor = LOG2E / head_dim**0.5
    starts = [pl.multiple_of(cols_ref[row, s] * TILE, TILE) for s in range(slots)]
    mixed = []
    for h in range(heads):
        lanes = slice(h * wide, (h + 1) * wide)
        kv = jnp.concatenate([kv_ref[pl.ds(s, TILE), lanes] for s in starts], axis=0)
        scores = lax.dot_general(
            q_ref[:, lanes], kv, (((1,), (1,)), ((), ())), preferred_element_type=jnp.float32
        )
        top = jnp.max(scores, axis=-1, keepdims=True)
        weights = jnp.exp2((scores - top) * factor)
        denom = jnp.sum(weights, axis=-1, keepdims=True)
        summed = jnp.dot(weights.astype(jnp.bfloat16), kv, preferred_element_type=jnp.float32)
        mixed.append((summed / denom)[:, head_dim:])
    out_ref[...] = jnp.concatenate(mixed, axis=1).astype(out_ref.dtype)


def attend(cols, queries, kv, heads, head_dim):
    rows = queries.shape[0]
    grid_spec = pltpu.PrefetchScalarGridSpec(
        num_scalar_prefetch=1,
        grid=(rows // TILE,),
        in_specs=[
            pl.BlockSpec((TILE, queries.shape[1]), lambda i, c: (i, 0)),
            pl.BlockSpec(memory_space=pltpu.VMEM),
        ],
        out_specs=pl.BlockSpec((TILE, heads * head_dim), lambda i, c: (i, 0)),
    )
    return pl.pallas_call(
        functools.partial(attend_kernel, heads, head_dim),
        grid_spec=grid_spec,
        out_shape=jax.ShapeDtypeStruct((rows, heads * head_dim), jnp.bfloat16),
        compiler_params=pltpu.CompilerParams(vmem_limit_bytes=48 * 2**20),
    )(cols, queries, kv)


def project(feats, weight):
    return jnp.dot(feats, weight, preferred_element_type=jnp.float32).astype(jnp.bfloat16)


def per_device(node_feats, w_qkv, w_out, tile_cols):
    width, heads, packed = w_qkv.shape
    head_dim = packed // 3
    feats = lax.all_gather(node_feats, "group", axis=0, tiled=True)
    w_q = jnp.pad(w_qkv[:, :, :head_dim], ((0, 0), (0, 0), (0, head_dim)))
    w_q = w_q.reshape(width, heads * 2 * head_dim)
    w_kv = w_qkv[:, :, head_dim:].reshape(width, heads * 2 * head_dim)
    kv = lax.all_gather(project(feats, w_kv), "loop", axis=0, tiled=True)
    queries = project(feats, w_q)
    w_full = lax.all_gather(w_out, "group", axis=0, tiled=True)
    mixed = attend(tile_cols, queries, kv, heads, head_dim)
    mixed = lax.all_to_all(mixed, "group", split_axis=0, concat_axis=1, tiled=True)
    return jnp.dot(mixed, w_full, preferred_element_type=jnp.float32).astype(jnp.bfloat16)


def solution(mesh):
    placed = (P(("loop", "group"), None), P(None, "group", None), P("group", None), P("loop", None))
    return jax.shard_map(
        per_device,
        mesh=mesh,
        in_specs=placed,
        out_specs=P(("loop", "group"), None),
        check_vma=False,
    )
```

```python
import functools

import jax
import jax.numpy as jnp
from jax import lax
from jax.experimental import pallas as pl
from jax.experimental.pallas import tpu as pltpu
from jax.sharding import PartitionSpec as P

TILE = 128
MESH = pl.DeviceIdType.MESH
LOG2E = 1.4426950408889634


def attend_kernel(heads, head_dim, cols_ref, q_ref, kv_ref, out_ref):
    row = pl.program_id(0)
    slots = cols_ref.shape[1]
    wide = 2 * head_dim
    factor = LOG2E / head_dim**0.5
    starts = [pl.multiple_of(cols_ref[row, s] * TILE, TILE) for s in range(slots)]
    mixed = []
    for h in range(heads):
        lanes = slice(h * wide, (h + 1) * wide)
        kv = jnp.concatenate([kv_ref[pl.ds(s, TILE), lanes] for s in starts], axis=0)
        scores = lax.dot_general(
            q_ref[:, lanes], kv, (((1,), (1,)), ((), ())), preferred_element_type=jnp.float32
        )
        top = jnp.max(scores, axis=-1, keepdims=True)
        weights = jnp.exp2((scores - top) * factor)
        denom = jnp.sum(weights, axis=-1, keepdims=True)
        summed = jnp.dot(weights.astype(jnp.bfloat16), kv, preferred_element_type=jnp.float32)
        mixed.append((summed / denom)[:, head_dim:])
    out_ref[...] = jnp.concatenate(mixed, axis=1).astype(out_ref.dtype)


def attend(cols, queries, kv, heads, head_dim):
    rows = queries.shape[0]
    grid_spec = pltpu.PrefetchScalarGridSpec(
        num_scalar_prefetch=1,
        grid=(rows // TILE,),
        in_specs=[
            pl.BlockSpec((TILE, queries.shape[1]), lambda i, c: (i, 0)),
            pl.BlockSpec(memory_space=pltpu.VMEM),
        ],
        out_specs=pl.BlockSpec((TILE, heads * head_dim), lambda i, c: (i, 0)),
    )
    return pl.pallas_call(
        functools.partial(attend_kernel, heads, head_dim),
        grid_spec=grid_spec,
        out_shape=jax.ShapeDtypeStruct((rows, heads * head_dim), jnp.bfloat16),
        compiler_params=pltpu.CompilerParams(vmem_limit_bytes=48 * 2**20),
    )(cols, queries, kv)


def gather_kernel(
    n_loop, n_group, feats_ref, w_ref, w_out_ref, kv_ref, q_ref, w_full_ref, arrived, own,
    feat_send, feat_recv, wout_send, wout_recv, up_send, up_recv, down_send, down_recv,
    sib_send, sib_recv, keep_sem, keep_w_sem,
):
    me, g = lax.axis_index("loop"), lax.axis_index("group")
    core, z = me % 2, me // 2
    chips = n_loop // 2
    sib = me + 1 - 2 * core
    has_up, has_down = z < chips - 1, z > 0
    rows, wide = own.shape[1], own.shape[2]
    cut = w_out_ref.shape[0]

    barrier = pltpu.get_barrier_semaphore()

    def greet(device):
        pl.semaphore_signal(barrier, inc=1, device_id=device, device_id_type=MESH)

    for j in range(1, n_group):
        greet((me, (g + j) % n_group))
    greet((sib, g))
    pl.when(has_up)(lambda: greet((me + 2, g)))
    pl.when(has_down)(lambda: greet((me - 2, g)))
    greetings = n_group + jnp.where(has_up, 1, 0) + jnp.where(has_down, 1, 0)
    pl.semaphore_wait(barrier, greetings)

    def remote(src, dst, send, recv, device):
        return pltpu.make_async_remote_copy(
            src_ref=src, dst_ref=dst, send_sem=send, recv_sem=recv,
            device_id=device, device_id_type=MESH,
        )

    def feat_copy(j):
        return remote(
            feats_ref, arrived.at[n_group - j - 1], feat_send.at[j - 1],
            feat_recv.at[n_group - j - 1], (me, (g + j) % n_group),
        )

    def wout_copy(j, owner):
        part = w_full_ref.at[pl.ds(pl.multiple_of(owner * cut, cut), cut)]
        return remote(
            w_out_ref, part, wout_send.at[j - 1], wout_recv.at[n_group - j - 1],
            (me, (g + j) % n_group),
        )

    def up_copy(src, block, k, s):
        dst = kv_ref.at[block, (g + k) % n_group]
        return remote(
            dst if src is None else src, dst, up_send.at[s, k], up_recv.at[s, k], (me + 2, g)
        )

    def down_copy(src, block, k, s):
        dst = kv_ref.at[block, (g + k) % n_group]
        return remote(
            dst if src is None else src, dst, down_send.at[s, k], down_recv.at[s, k], (me - 2, g)
        )

    def sib_copy(src, block, k, role):
        dst = kv_ref.at[block, (g + k) % n_group]
        return remote(
            dst if src is None else src, dst, sib_send.at[role, k], sib_recv.at[role, k], (sib, g)
        )

    def keep_copy(k):
        return pltpu.make_async_copy(
            own.at[k], kv_ref.at[me, (g + k) % n_group], keep_sem.at[k]
        )

    for j in range(1, n_group):
        feat_copy(j).start()

    def own_piece(k):
        if k:
            feat_copy(n_group - k).wait_recv()
        source = feats_ref if k == 0 else arrived.at[k - 1]
        base = pl.multiple_of(((g + k) % n_group) * rows, rows)
        step = 256

        @pl.loop(0, rows // step)
        def _(i):
            at = pl.multiple_of(i * step, step)
            both = jnp.dot(
                source[pl.ds(at, step), :], w_ref[...], preferred_element_type=jnp.float32
            ).astype(jnp.bfloat16)
            q_ref[pl.ds(pl.multiple_of(base + at, step), step), :] = both[:, :wide]
            own[k, pl.ds(at, step), :] = both[:, wide:]

        pl.when(has_up)(lambda: up_copy(own.at[k], me, k, 0).start())
        pl.when(has_down)(lambda: down_copy(own.at[k], me, k, 0).start())
        sib_copy(own.at[k], me, k, 0).start()
        keep_copy(k).start()

    def arrival(k, s):
        @pl.when(z - 1 - s >= 0)
        def _():
            block = me - 2 * (1 + s)
            up_copy(None, block, k, s).wait_recv()
            if s + 1 < chips - 1:
                pl.when(has_up)(lambda: up_copy(None, block, k, s + 1).start())
            sib_copy(None, block, k, 1 + s).start()

        @pl.when(z + 1 + s < chips)
        def _():
            block = me + 2 * (1 + s)
            down_copy(None, block, k, s).wait_recv()
            if s + 1 < chips - 1:
                pl.when(has_down)(lambda: down_copy(None, block, k, s + 1).start())
            sib_copy(None, block, k, chips + s).start()

    for t in range(n_group + chips - 1):
        if t < n_group:
            own_piece(t)
        if t == n_group - 1:
            for j in range(1, n_group):
                wout_copy(j, g).start()
            keep_w = pltpu.make_async_copy(
                w_out_ref, w_full_ref.at[pl.ds(pl.multiple_of(g * cut, cut), cut)], keep_w_sem
            )
            keep_w.start()
        for s in range(chips - 1):
            if 0 <= t - 1 - s < n_group:
                arrival(t - 1 - s, s)

    keep_w.wait()
    for j in range(1, n_group):
        feat_copy(j).wait_send()
        wout_copy(j, g).wait_send()
        wout_copy(n_group - j, (g + j) % n_group).wait_recv()
    for k in range(n_group):
        keep_copy(k).wait()
        mine = sib_copy(own.at[k], me, k, 0)
        mine.wait_send()
        sib_copy(None, sib, k, 0).wait_recv()
        for s in range(chips - 1):

            @pl.when(z - 1 - s >= 0)
            def _():
                sib_copy(None, me - 2 * (1 + s), k, 1 + s).wait_send()
                sib_copy(None, sib - 2 * (1 + s), k, 1 + s).wait_recv()

            @pl.when(z + 1 + s < chips)
            def _():
                sib_copy(None, me + 2 * (1 + s), k, chips + s).wait_send()
                sib_copy(None, sib + 2 * (1 + s), k, chips + s).wait_recv()

            @pl.when(has_up & (z - s >= 0))
            def _():
                up_copy(own.at[k] if s == 0 else None, me - 2 * s, k, s).wait_send()

            @pl.when(has_down & (z + s < chips))
            def _():
                down_copy(own.at[k] if s == 0 else None, me + 2 * s, k, s).wait_send()


def gather(feats, weight, w_out, n_loop, n_group):
    rows, width = feats.shape
    wide = weight.shape[1] // 2
    chips = n_loop // 2
    vmem, anywhere = pl.BlockSpec(memory_space=pltpu.VMEM), pl.BlockSpec(memory_space=pl.ANY)
    dma = pltpu.SemaphoreType.DMA
    return pl.pallas_call(
        functools.partial(gather_kernel, n_loop, n_group),
        in_specs=[vmem, vmem, anywhere],
        out_specs=[anywhere, vmem, anywhere],
        out_shape=[
            jax.ShapeDtypeStruct((n_loop, n_group, rows, wide), jnp.bfloat16),
            jax.ShapeDtypeStruct((n_group * rows, wide), jnp.bfloat16),
            jax.ShapeDtypeStruct((n_group * w_out.shape[0], w_out.shape[1]), jnp.bfloat16),
        ],
        scratch_shapes=[
            pltpu.VMEM((n_group - 1, rows, width), jnp.bfloat16),
            pltpu.VMEM((n_group, rows, wide), jnp.bfloat16),
            dma((n_group - 1,)), dma((n_group - 1,)),
            dma((n_group - 1,)), dma((n_group - 1,)),
            dma((chips - 1, n_group)), dma((chips - 1, n_group)),
            dma((chips - 1, n_group)), dma((chips - 1, n_group)),
            dma((2 * chips - 1, n_group)), dma((2 * chips - 1, n_group)),
            dma((n_group,)), dma(()),
        ],
        compiler_params=pltpu.CompilerParams(
            collective_id=0, has_side_effects=True, vmem_limit_bytes=48 * 2**20
        ),
    )(feats, weight, w_out)


def per_device(node_feats, w_qkv, w_out, tile_cols):
    width, heads, packed = w_qkv.shape
    head_dim = packed // 3
    n_loop, n_group = lax.axis_size("loop"), lax.axis_size("group")
    w_q = jnp.pad(w_qkv[:, :, :head_dim], ((0, 0), (0, 0), (0, head_dim)))
    w_q = w_q.reshape(width, heads * 2 * head_dim)
    w_kv = w_qkv[:, :, head_dim:].reshape(width, heads * 2 * head_dim)
    weight = jnp.concatenate([w_q, w_kv], axis=1)
    kv, queries, w_full = gather(node_feats, weight, w_out, n_loop, n_group)
    kv = kv.reshape(-1, kv.shape[-1])
    mixed = attend(tile_cols, queries, kv, heads, head_dim)
    mixed = lax.all_to_all(mixed, "group", split_axis=0, concat_axis=1, tiled=True)
    return jnp.dot(mixed, w_full, preferred_element_type=jnp.float32).astype(jnp.bfloat16)


def solution(mesh):
    placed = (P(("loop", "group"), None), P(None, "group", None), P("group", None), P("loop", None))
    return jax.shard_map(
        per_device,
        mesh=mesh,
        in_specs=placed,
        out_specs=P(("loop", "group"), None),
        check_vma=False,
    )
```

```python
import functools

import jax
import jax.numpy as jnp
from jax import lax
from jax.experimental import pallas as pl
from jax.experimental.pallas import tpu as pltpu
from jax.sharding import PartitionSpec as P

TILE = 128
MESH = pl.DeviceIdType.MESH
LOG2E = 1.4426950408889634


def attend_kernel(heads, head_dim, cols_ref, q_ref, kv_ref, out_ref):
    row = pl.program_id(0)
    slots = cols_ref.shape[1]
    wide = 2 * head_dim
    factor = LOG2E / head_dim**0.5
    starts = [pl.multiple_of(cols_ref[row, s] * TILE, TILE) for s in range(slots)]
    mixed = []
    for h in range(heads):
        lanes = slice(h * wide, (h + 1) * wide)
        kv = jnp.concatenate([kv_ref[pl.ds(s, TILE), lanes] for s in starts], axis=0)
        scores = lax.dot_general(
            q_ref[:, lanes], kv, (((1,), (1,)), ((), ())), preferred_element_type=jnp.float32
        )
        top = jnp.max(scores, axis=-1, keepdims=True)
        weights = jnp.exp2((scores - top) * factor)
        denom = jnp.sum(weights, axis=-1, keepdims=True)
        summed = jnp.dot(weights.astype(jnp.bfloat16), kv, preferred_element_type=jnp.float32)
        mixed.append((summed / denom)[:, head_dim:])
    out_ref[...] = jnp.concatenate(mixed, axis=1).astype(out_ref.dtype)


def attend(cols, queries, kv, heads, head_dim):
    rows = queries.shape[0]
    grid_spec = pltpu.PrefetchScalarGridSpec(
        num_scalar_prefetch=1,
        grid=(rows // TILE,),
        in_specs=[
            pl.BlockSpec((TILE, queries.shape[1]), lambda i, c: (i, 0)),
            pl.BlockSpec(memory_space=pltpu.VMEM),
        ],
        out_specs=pl.BlockSpec((TILE, heads * head_dim), lambda i, c: (i, 0)),
    )
    return pl.pallas_call(
        functools.partial(attend_kernel, heads, head_dim),
        grid_spec=grid_spec,
        out_shape=jax.ShapeDtypeStruct((rows, heads * head_dim), jnp.bfloat16),
        compiler_params=pltpu.CompilerParams(vmem_limit_bytes=48 * 2**20),
    )(cols, queries, kv)


def gather_kernel(
    n_loop, n_group, feats_ref, w_ref, w_out_ref, kv_ref, q_ref, w_full_ref, arrived, own,
    feat_send, feat_recv, wout_send, wout_recv, up_send, up_recv, down_send, down_recv,
    sib_send, sib_recv, keep_sem, keep_w_sem,
    far_feats, far_own, far_send, far_recv, far_sib_send, far_sib_recv, far_keep_sem,
):
    me, g = lax.axis_index("loop"), lax.axis_index("group")
    core, z = me % 2, me // 2
    chips = n_loop // 2
    sib = me + 1 - 2 * core
    has_up, has_down = z < chips - 1, z > 0
    at_end = (z == 0) | (z == chips - 1)
    across = 2 * (chips - 1 - z) + core
    rows, wide = own.shape[1], own.shape[2]
    cut = w_out_ref.shape[0]

    barrier = pltpu.get_barrier_semaphore()

    def greet(device):
        pl.semaphore_signal(barrier, inc=1, device_id=device, device_id_type=MESH)

    for j in range(1, n_group):
        greet((me, (g + j) % n_group))
    greet((sib, g))
    pl.when(has_up)(lambda: greet((me + 2, g)))
    pl.when(has_down)(lambda: greet((me - 2, g)))
    pl.when(at_end)(lambda: greet((across, g)))
    greetings = n_group + jnp.where(at_end, 1, 0) + jnp.where(has_up, 1, 0) + jnp.where(has_down, 1, 0)
    pl.semaphore_wait(barrier, greetings)

    def remote(src, dst, send, recv, device):
        return pltpu.make_async_remote_copy(
            src_ref=src, dst_ref=dst, send_sem=send, recv_sem=recv,
            device_id=device, device_id_type=MESH,
        )

    def feat_copy(j):
        return remote(
            feats_ref, arrived.at[n_group - j - 1], feat_send.at[j - 1],
            feat_recv.at[n_group - j - 1], (me, (g + j) % n_group),
        )

    def wout_copy(j, owner):
        part = w_full_ref.at[pl.ds(pl.multiple_of(owner * cut, cut), cut)]
        return remote(
            w_out_ref, part, wout_send.at[j - 1], wout_recv.at[n_group - j - 1],
            (me, (g + j) % n_group),
        )

    def up_copy(src, block, k, s):
        dst = kv_ref.at[block, (g + k) % n_group]
        return remote(
            dst if src is None else src, dst, up_send.at[s, k], up_recv.at[s, k], (me + 2, g)
        )

    def down_copy(src, block, k, s):
        dst = kv_ref.at[block, (g + k) % n_group]
        return remote(
            dst if src is None else src, dst, down_send.at[s, k], down_recv.at[s, k], (me - 2, g)
        )

    def sib_copy(src, block, k, role):
        dst = kv_ref.at[block, (g + k) % n_group]
        return remote(
            dst if src is None else src, dst, sib_send.at[role, k], sib_recv.at[role, k], (sib, g)
        )

    def keep_copy(k):
        return pltpu.make_async_copy(
            own.at[k], kv_ref.at[me, (g + k) % n_group], keep_sem.at[k]
        )

    def across_copy():
        return remote(
            feats_ref, far_feats.at[0], far_send.at[0], far_recv.at[0], (across, g)
        )

    def far_copy(j):
        return remote(
            far_feats.at[0], far_feats.at[n_group - j], far_send.at[j],
            far_recv.at[n_group - j], (me, (g + j) % n_group),
        )

    def far_sib_copy(block, k):
        return remote(
            far_own.at[k], kv_ref.at[block, (g + k) % n_group],
            far_sib_send.at[k], far_sib_recv.at[k], (sib, g),
        )

    def far_keep_copy(k):
        return pltpu.make_async_copy(
            far_own.at[k], kv_ref.at[across, (g + k) % n_group], far_keep_sem.at[k]
        )

    def far_share():
        across_copy().wait_recv()
        for j in range(1, n_group):
            far_copy(j).start()

    def far_project():
        for k in range(n_group):
            if k:
                far_copy(n_group - k).wait_recv()
            step = 256

            @pl.loop(0, rows // step)
            def _(i):
                at = pl.multiple_of(i * step, step)
                far_own[k, pl.ds(at, step), :] = jnp.dot(
                    far_feats[k, pl.ds(at, step), :], w_ref[:, wide:],
                    preferred_element_type=jnp.float32,
                ).astype(jnp.bfloat16)

            far_sib_copy(across, k).start()
            far_keep_copy(k).start()

    def far_finish():
        across_copy().wait_send()
        for j in range(1, n_group):
            far_copy(j).wait_send()
        for k in range(n_group):
            far_keep_copy(k).wait()
            far_sib_copy(across, k).wait_send()
            far_sib_copy(across + 1 - 2 * core, k).wait_recv()

    for j in range(1, n_group):
        feat_copy(j).start()
    pl.when(at_end)(lambda: across_copy().start())

    def own_piece(k):
        if k:
            feat_copy(n_group - k).wait_recv()
        source = feats_ref if k == 0 else arrived.at[k - 1]
        base = pl.multiple_of(((g + k) % n_group) * rows, rows)
        step = 256

        @pl.loop(0, rows // step)
        def _(i):
            at = pl.multiple_of(i * step, step)
            both = jnp.dot(
                source[pl.ds(at, step), :], w_ref[...], preferred_element_type=jnp.float32
            ).astype(jnp.bfloat16)
            q_ref[pl.ds(pl.multiple_of(base + at, step), step), :] = both[:, :wide]
            own[k, pl.ds(at, step), :] = both[:, wide:]

        pl.when(has_up)(lambda: up_copy(own.at[k], me, k, 0).start())
        pl.when(has_down)(lambda: down_copy(own.at[k], me, k, 0).start())
        sib_copy(own.at[k], me, k, 0).start()
        keep_copy(k).start()

    def arrival(k, s):
        @pl.when(z - 1 - s >= 0)
        def _():
            block = me - 2 * (1 + s)
            up_copy(None, block, k, s).wait_recv()
            if s + 1 < chips - 2:
                pl.when(has_up)(lambda: up_copy(None, block, k, s + 1).start())
            sib_copy(None, block, k, 1 + s).start()

        @pl.when(z + 1 + s < chips)
        def _():
            block = me + 2 * (1 + s)
            down_copy(None, block, k, s).wait_recv()
            if s + 1 < chips - 2:
                pl.when(has_down)(lambda: down_copy(None, block, k, s + 1).start())
            sib_copy(None, block, k, chips + s).start()

    for t in range(n_group + chips - 2):
        if t < n_group:
            own_piece(t)
        if t == n_group - 1:
            for j in range(1, n_group):
                wout_copy(j, g).start()
            keep_w = pltpu.make_async_copy(
                w_out_ref, w_full_ref.at[pl.ds(pl.multiple_of(g * cut, cut), cut)], keep_w_sem
            )
            keep_w.start()
            pl.when(at_end)(far_share)
        for s in range(chips - 2):
            if 0 <= t - 1 - s < n_group:
                arrival(t - 1 - s, s)
        if t == n_group:
            pl.when(at_end)(far_project)

    keep_w.wait()
    for j in range(1, n_group):
        feat_copy(j).wait_send()
        wout_copy(j, g).wait_send()
        wout_copy(n_group - j, (g + j) % n_group).wait_recv()
    for k in range(n_group):
        keep_copy(k).wait()
        mine = sib_copy(own.at[k], me, k, 0)
        mine.wait_send()
        sib_copy(None, sib, k, 0).wait_recv()
        for s in range(chips - 2):

            @pl.when(z - 1 - s >= 0)
            def _():
                sib_copy(None, me - 2 * (1 + s), k, 1 + s).wait_send()
                sib_copy(None, sib - 2 * (1 + s), k, 1 + s).wait_recv()

            @pl.when(z + 1 + s < chips)
            def _():
                sib_copy(None, me + 2 * (1 + s), k, chips + s).wait_send()
                sib_copy(None, sib + 2 * (1 + s), k, chips + s).wait_recv()

            @pl.when(has_up & (z - s >= 0))
            def _():
                up_copy(own.at[k] if s == 0 else None, me - 2 * s, k, s).wait_send()

            @pl.when(has_down & (z + s < chips))
            def _():
                down_copy(own.at[k] if s == 0 else None, me + 2 * s, k, s).wait_send()

    pl.when(at_end)(far_finish)


def gather(feats, weight, w_out, n_loop, n_group):
    rows, width = feats.shape
    wide = weight.shape[1] // 2
    chips = n_loop // 2
    vmem, anywhere = pl.BlockSpec(memory_space=pltpu.VMEM), pl.BlockSpec(memory_space=pl.ANY)
    dma = pltpu.SemaphoreType.DMA
    return pl.pallas_call(
        functools.partial(gather_kernel, n_loop, n_group),
        in_specs=[vmem, vmem, anywhere],
        out_specs=[anywhere, vmem, anywhere],
        out_shape=[
            jax.ShapeDtypeStruct((n_loop, n_group, rows, wide), jnp.bfloat16),
            jax.ShapeDtypeStruct((n_group * rows, wide), jnp.bfloat16),
            jax.ShapeDtypeStruct((n_group * w_out.shape[0], w_out.shape[1]), jnp.bfloat16),
        ],
        scratch_shapes=[
            pltpu.VMEM((n_group - 1, rows, width), jnp.bfloat16),
            pltpu.VMEM((n_group, rows, wide), jnp.bfloat16),
            dma((n_group - 1,)), dma((n_group - 1,)),
            dma((n_group - 1,)), dma((n_group - 1,)),
            dma((chips - 1, n_group)), dma((chips - 1, n_group)),
            dma((chips - 1, n_group)), dma((chips - 1, n_group)),
            dma((2 * chips - 1, n_group)), dma((2 * chips - 1, n_group)),
            dma((n_group,)), dma(()),
            pltpu.VMEM((n_group, rows, width), jnp.bfloat16),
            pltpu.VMEM((n_group, rows, wide), jnp.bfloat16),
            dma((n_group,)), dma((n_group,)), dma((n_group,)), dma((n_group,)), dma((n_group,)),
        ],
        compiler_params=pltpu.CompilerParams(
            collective_id=0, has_side_effects=True, vmem_limit_bytes=48 * 2**20
        ),
    )(feats, weight, w_out)


def per_device(node_feats, w_qkv, w_out, tile_cols):
    width, heads, packed = w_qkv.shape
    head_dim = packed // 3
    n_loop, n_group = lax.axis_size("loop"), lax.axis_size("group")
    w_q = jnp.pad(w_qkv[:, :, :head_dim], ((0, 0), (0, 0), (0, head_dim)))
    w_q = w_q.reshape(width, heads * 2 * head_dim)
    w_kv = w_qkv[:, :, head_dim:].reshape(width, heads * 2 * head_dim)
    weight = jnp.concatenate([w_q, w_kv], axis=1)
    kv, queries, w_full = gather(node_feats, weight, w_out, n_loop, n_group)
    kv = kv.reshape(-1, kv.shape[-1])
    mixed = attend(tile_cols, queries, kv, heads, head_dim)
    mixed = lax.all_to_all(mixed, "group", split_axis=0, concat_axis=1, tiled=True)
    return jnp.dot(mixed, w_full, preferred_element_type=jnp.float32).astype(jnp.bfloat16)


def solution(mesh):
    placed = (P(("loop", "group"), None), P(None, "group", None), P("group", None), P("loop", None))
    return jax.shard_map(
        per_device,
        mesh=mesh,
        in_specs=placed,
        out_specs=P(("loop", "group"), None),
        check_vma=False,
    )
```

```python
import functools

import jax
import jax.numpy as jnp
from jax import lax
from jax.experimental import pallas as pl
from jax.experimental.pallas import tpu as pltpu
from jax.sharding import PartitionSpec as P

TILE = 128
MESH = pl.DeviceIdType.MESH
LOG2E = 1.4426950408889634


def attend_tile(cols_ref, row, queries, kv_ref, heads, head_dim):
    slots = cols_ref.shape[1]
    wide = 2 * head_dim
    factor = LOG2E / head_dim**0.5
    tiles = [cols_ref[row, s] for s in range(slots)]
    mixed = []
    for h in range(heads):
        lanes = slice(h * wide, (h + 1) * wide)
        kv = jnp.concatenate([kv_ref[t, :, lanes] for t in tiles], axis=0)
        scores = lax.dot_general(
            queries[:, lanes], kv, (((1,), (1,)), ((), ())), preferred_element_type=jnp.float32
        )
        top = jnp.max(scores, axis=-1, keepdims=True)
        weights = jnp.exp2((scores - top) * factor)
        denom = jnp.sum(weights, axis=-1, keepdims=True)
        summed = jnp.dot(weights.astype(jnp.bfloat16), kv, preferred_element_type=jnp.float32)
        mixed.append((summed / denom)[:, head_dim:])
    return jnp.concatenate(mixed, axis=1).astype(jnp.bfloat16)


def fused_kernel(
    n_loop, n_group, heads, head_dim,
    cols_ref, feats_ref, w_ref, w_out_ref, out_ref, kv_ref, q_ref, w_full_ref, arrived,
    feat_send, feat_recv, wout_send, wout_recv, up_send, up_recv, down_send, down_recv,
    sib_send, sib_recv, far_feats, far_send, far_recv, far_sib_send, far_sib_recv,
    mine, landed, mix_send, mix_recv,
):
    me, g = lax.axis_index("loop"), lax.axis_index("group")
    core, z = me % 2, me // 2
    chips = n_loop // 2
    sib = me + 1 - 2 * core
    has_up, has_down = z < chips - 1, z > 0
    at_end = (z == 0) | (z == chips - 1)
    across = 2 * (chips - 1 - z) + core
    rows, wide = feats_ref.shape[0], kv_ref.shape[2]
    cut = w_out_ref.shape[0]

    barrier = pltpu.get_barrier_semaphore()

    def greet(device):
        pl.semaphore_signal(barrier, inc=1, device_id=device, device_id_type=MESH)

    for j in range(1, n_group):
        greet((me, (g + j) % n_group))
    greet((sib, g))
    pl.when(has_up)(lambda: greet((me + 2, g)))
    pl.when(has_down)(lambda: greet((me - 2, g)))
    pl.when(at_end)(lambda: greet((across, g)))
    greetings = n_group + jnp.where(at_end, 1, 0) + jnp.where(has_up, 1, 0) + jnp.where(has_down, 1, 0)
    pl.semaphore_wait(barrier, greetings)

    def remote(src, dst, send, recv, device):
        return pltpu.make_async_remote_copy(
            src_ref=src, dst_ref=dst, send_sem=send, recv_sem=recv,
            device_id=device, device_id_type=MESH,
        )

    def place(block, k):
        return (block * n_group + (g + k) % n_group) * (rows // TILE)

    def piece(block, k):
        return kv_ref.at[pl.ds(place(block, k), rows // TILE)]

    def feat_copy(j):
        return remote(
            feats_ref, arrived.at[n_group - j - 1], feat_send.at[j - 1],
            feat_recv.at[n_group - j - 1], (me, (g + j) % n_group),
        )

    def wout_copy(j, owner):
        part = w_full_ref.at[pl.ds(pl.multiple_of(owner * cut, cut), cut)]
        return remote(
            w_out_ref, part, wout_send.at[j - 1], wout_recv.at[n_group - j - 1],
            (me, (g + j) % n_group),
        )

    def up_copy(block, k, s):
        at = piece(block, k)
        return remote(at, at, up_send.at[s, k], up_recv.at[s, k], (me + 2, g))

    def down_copy(block, k, s):
        at = piece(block, k)
        return remote(at, at, down_send.at[s, k], down_recv.at[s, k], (me - 2, g))

    def sib_copy(block, k, role):
        at = piece(block, k)
        return remote(at, at, sib_send.at[role, k], sib_recv.at[role, k], (sib, g))

    def across_copy():
        return remote(
            feats_ref, far_feats.at[0], far_send.at[0], far_recv.at[0], (across, g)
        )

    def far_copy(j):
        return remote(
            far_feats.at[0], far_feats.at[n_group - j], far_send.at[j],
            far_recv.at[n_group - j], (me, (g + j) % n_group),
        )

    def far_sib_copy(block, k):
        at = piece(block, k)
        return remote(at, at, far_sib_send.at[k], far_sib_recv.at[k], (sib, g))

    def far_share():
        across_copy().wait_recv()
        for j in range(1, n_group):
            far_copy(j).start()

    def far_project():
        for k in range(n_group):
            if k:
                far_copy(n_group - k).wait_recv()
            step = 256

            @pl.loop(0, rows // step)
            def _(i):
                at = pl.multiple_of(i * step, step)
                found = jnp.dot(
                    far_feats[k, pl.ds(at, step), :], w_ref[:, wide:],
                    preferred_element_type=jnp.float32,
                ).astype(jnp.bfloat16)
                for m in range(step // TILE):
                    tile = place(across, k) + i * (step // TILE) + m
                    kv_ref[tile] = found[m * TILE : (m + 1) * TILE]

            far_sib_copy(across, k).start()

    def far_finish():
        across_copy().wait_send()
        for j in range(1, n_group):
            far_copy(j).wait_send()
        for k in range(n_group):
            far_sib_copy(across, k).wait_send()
            far_sib_copy(across + 1 - 2 * core, k).wait_recv()

    for j in range(1, n_group):
        feat_copy(j).start()
    pl.when(at_end)(lambda: across_copy().start())

    def own_piece(k):
        if k:
            feat_copy(n_group - k).wait_recv()
        source = feats_ref if k == 0 else arrived.at[k - 1]
        base = pl.multiple_of(((g + k) % n_group) * rows, rows)
        step = 256

        @pl.loop(0, rows // step)
        def _(i):
            at = pl.multiple_of(i * step, step)
            both = jnp.dot(
                source[pl.ds(at, step), :], w_ref[...], preferred_element_type=jnp.float32
            ).astype(jnp.bfloat16)
            q_ref[pl.ds(pl.multiple_of(base + at, step), step), :] = both[:, :wide]
            for m in range(step // TILE):
                tile = place(me, k) + i * (step // TILE) + m
                kv_ref[tile] = both[m * TILE : (m + 1) * TILE, wide:]

        pl.when(has_up)(lambda: up_copy(me, k, 0).start())
        pl.when(has_down)(lambda: down_copy(me, k, 0).start())
        sib_copy(me, k, 0).start()

    def arrival(k, s):
        @pl.when(z - 1 - s >= 0)
        def _():
            block = me - 2 * (1 + s)
            up_copy(block, k, s).wait_recv()
            if s + 1 < chips - 2:
                pl.when(has_up)(lambda: up_copy(block, k, s + 1).start())
            sib_copy(block, k, 1 + s).start()

        @pl.when(z + 1 + s < chips)
        def _():
            block = me + 2 * (1 + s)
            down_copy(block, k, s).wait_recv()
            if s + 1 < chips - 2:
                pl.when(has_down)(lambda: down_copy(block, k, s + 1).start())
            sib_copy(block, k, chips + s).start()

    for t in range(n_group + chips - 2):
        if t < n_group:
            own_piece(t)
        if t == n_group - 1:
            for j in range(1, n_group):
                wout_copy(j, g).start()
            w_full_ref[pl.ds(pl.multiple_of(g * cut, cut), cut), :] = w_out_ref[...]
            pl.when(at_end)(far_share)
        for s in range(chips - 2):
            if 0 <= t - 1 - s < n_group:
                arrival(t - 1 - s, s)
        if t == n_group:
            pl.when(at_end)(far_project)

    for j in range(1, n_group):
        feat_copy(j).wait_send()
        wout_copy(j, g).wait_send()
        wout_copy(n_group - j, (g + j) % n_group).wait_recv()
    for k in range(n_group):
        sib_copy(me, k, 0).wait_send()
        sib_copy(sib, k, 0).wait_recv()
        for s in range(chips - 2):

            @pl.when(z - 1 - s >= 0)
            def _():
                sib_copy(me - 2 * (1 + s), k, 1 + s).wait_send()
                sib_copy(sib - 2 * (1 + s), k, 1 + s).wait_recv()

            @pl.when(z + 1 + s < chips)
            def _():
                sib_copy(me + 2 * (1 + s), k, chips + s).wait_send()
                sib_copy(sib + 2 * (1 + s), k, chips + s).wait_recv()

            @pl.when(has_up & (z - s >= 0))
            def _():
                up_copy(me - 2 * s, k, s).wait_send()

            @pl.when(has_down & (z + s < chips))
            def _():
                down_copy(me + 2 * s, k, s).wait_send()

    pl.when(at_end)(far_finish)

    def mix_copy(j, slot):
        return remote(
            mine.at[j - 1], landed.at[slot], mix_send.at[j - 1],
            mix_recv.at[n_group - j - 1], (me, (g + j) % n_group),
        )

    for j in [*range(1, n_group), 0]:
        first = ((g + j) % n_group) * (rows // TILE)

        @pl.loop(0, rows // TILE)
        def _(i):
            row = first + i
            at = pl.multiple_of(i * TILE, TILE)
            queries = q_ref[pl.ds(pl.multiple_of(row * TILE, TILE), TILE), :]
            mixed = attend_tile(cols_ref, row, queries, kv_ref, heads, head_dim)
            if j:
                mine[j - 1, pl.ds(at, TILE), :] = mixed
            else:
                landed[g, pl.ds(at, TILE), :] = mixed

        if j:
            mix_copy(j, g).start()

    for j in range(1, n_group):
        mix_copy(j, g).wait_send()
        mix_copy(n_group - j, (g + j) % n_group).wait_recv()

    @pl.loop(0, rows // 256)
    def _(i):
        at = pl.ds(pl.multiple_of(i * 256, 256), 256)
        mixed = jnp.concatenate([landed[m, at, :] for m in range(n_group)], axis=1)
        out_ref[at, :] = jnp.dot(
            mixed, w_full_ref[...], preferred_element_type=jnp.float32
        ).astype(out_ref.dtype)


def fused(cols, feats, weight, w_out, n_loop, n_group, heads, head_dim):
    rows, width = feats.shape
    wide = weight.shape[1] // 2
    chips = n_loop // 2
    vmem, dma = pl.BlockSpec(memory_space=pltpu.VMEM), pltpu.SemaphoreType.DMA
    return pl.pallas_call(
        functools.partial(fused_kernel, n_loop, n_group, heads, head_dim),
        in_specs=[pl.BlockSpec(memory_space=pltpu.SMEM), vmem, vmem, vmem],
        out_specs=vmem,
        out_shape=jax.ShapeDtypeStruct((rows, w_out.shape[1]), jnp.bfloat16),
        scratch_shapes=[
            pltpu.VMEM((n_loop * n_group * rows // TILE, TILE, wide), jnp.bfloat16),
            pltpu.VMEM((n_group * rows, wide), jnp.bfloat16),
            pltpu.VMEM((n_group * w_out.shape[0], w_out.shape[1]), jnp.bfloat16),
            pltpu.VMEM((n_group - 1, rows, width), jnp.bfloat16),
            dma((n_group - 1,)), dma((n_group - 1,)),
            dma((n_group - 1,)), dma((n_group - 1,)),
            dma((chips - 1, n_group)), dma((chips - 1, n_group)),
            dma((chips - 1, n_group)), dma((chips - 1, n_group)),
            dma((2 * chips - 1, n_group)), dma((2 * chips - 1, n_group)),
            pltpu.VMEM((n_group, rows, width), jnp.bfloat16),
            dma((n_group,)), dma((n_group,)), dma((n_group,)), dma((n_group,)),
            pltpu.VMEM((n_group - 1, rows, heads * head_dim), jnp.bfloat16),
            pltpu.VMEM((n_group, rows, heads * head_dim), jnp.bfloat16),
            dma((n_group - 1,)), dma((n_group - 1,)),
        ],
        compiler_params=pltpu.CompilerParams(
            collective_id=0, has_side_effects=True, vmem_limit_bytes=56 * 2**20
        ),
    )(cols, feats, weight, w_out)


def per_device(node_feats, w_qkv, w_out, tile_cols):
    width, heads, packed = w_qkv.shape
    head_dim = packed // 3
    n_loop, n_group = lax.axis_size("loop"), lax.axis_size("group")
    w_q = jnp.pad(w_qkv[:, :, :head_dim], ((0, 0), (0, 0), (0, head_dim)))
    w_q = w_q.reshape(width, heads * 2 * head_dim)
    w_kv = w_qkv[:, :, head_dim:].reshape(width, heads * 2 * head_dim)
    weight = jnp.concatenate([w_q, w_kv], axis=1)
    return fused(tile_cols, node_feats, weight, w_out, n_loop, n_group, heads, head_dim)


def solution(mesh):
    placed = (P(("loop", "group"), None), P(None, "group", None), P("group", None), P("loop", None))
    return jax.shard_map(
        per_device,
        mesh=mesh,
        in_specs=placed,
        out_specs=P(("loop", "group"), None),
        check_vma=False,
    )
```

```python
import functools

import jax
import jax.numpy as jnp
from jax import lax
from jax.experimental import pallas as pl
from jax.experimental.pallas import tpu as pltpu
from jax.sharding import PartitionSpec as P

TILE = 128
MESH = pl.DeviceIdType.MESH
LOG2E = 1.4426950408889634


def attend_tile(cols_ref, row, queries, kv_ref, heads, head_dim):
    slots = cols_ref.shape[1]
    wide = 2 * head_dim
    factor = LOG2E / head_dim**0.5
    tiles = [cols_ref[row, s] for s in range(slots)]
    mixed = []
    for h in range(heads):
        lanes = slice(h * wide, (h + 1) * wide)
        kv = jnp.concatenate([kv_ref[t, :, lanes] for t in tiles], axis=0)
        scores = lax.dot_general(
            queries[:, lanes], kv, (((1,), (1,)), ((), ())), preferred_element_type=jnp.float32
        )
        top = jnp.max(scores, axis=-1, keepdims=True)
        weights = jnp.exp2((scores - top) * factor)
        denom = jnp.sum(weights, axis=-1, keepdims=True)
        summed = jnp.dot(weights.astype(jnp.bfloat16), kv, preferred_element_type=jnp.float32)
        mixed.append((summed / denom)[:, head_dim:])
    return jnp.concatenate(mixed, axis=1).astype(jnp.bfloat16)


def fused_kernel(
    n_loop, n_group, heads, head_dim,
    cols_ref, feats_ref, w_ref, w_out_ref, out_ref, kv_ref, q_ref, w_full_ref, arrived,
    feat_send, feat_recv, wout_send, wout_recv, up_send, up_recv, down_send, down_recv,
    sib_send, sib_recv, far_feats, far_send, far_recv, far_sib_send, far_sib_recv,
    mine, landed, mix_send, mix_recv,
):
    me, g = lax.axis_index("loop"), lax.axis_index("group")
    core, z = me % 2, me // 2
    chips = n_loop // 2
    sib = me + 1 - 2 * core
    has_up, has_down = z < chips - 1, z > 0
    at_end = (z == 0) | (z == chips - 1)
    across = 2 * (chips - 1 - z) + core
    rows, wide = feats_ref.shape[0], kv_ref.shape[2]
    cut = w_out_ref.shape[0]

    barrier = pltpu.get_barrier_semaphore()

    def greet(device):
        pl.semaphore_signal(barrier, inc=1, device_id=device, device_id_type=MESH)

    for j in range(1, n_group):
        greet((me, (g + j) % n_group))
    greet((sib, g))
    pl.when(has_up)(lambda: greet((me + 2, g)))
    pl.when(has_down)(lambda: greet((me - 2, g)))
    pl.when(at_end)(lambda: greet((across, g)))
    greetings = n_group + jnp.where(at_end, 1, 0) + jnp.where(has_up, 1, 0) + jnp.where(has_down, 1, 0)
    pl.semaphore_wait(barrier, greetings)

    def remote(src, dst, send, recv, device):
        return pltpu.make_async_remote_copy(
            src_ref=src, dst_ref=dst, send_sem=send, recv_sem=recv,
            device_id=device, device_id_type=MESH,
        )

    def place(block, k):
        return (block * n_group + (g + k) % n_group) * (rows // TILE)

    def piece(block, k):
        return kv_ref.at[pl.ds(place(block, k), rows // TILE)]

    def feat_copy(j):
        return remote(
            feats_ref, arrived.at[n_group - j - 1], feat_send.at[j - 1],
            feat_recv.at[n_group - j - 1], (me, (g + j) % n_group),
        )

    def wout_copy(j, owner):
        part = w_full_ref.at[pl.ds(pl.multiple_of(owner * cut, cut), cut)]
        return remote(
            w_out_ref, part, wout_send.at[j - 1], wout_recv.at[n_group - j - 1],
            (me, (g + j) % n_group),
        )

    def up_copy(block, k, s):
        at = piece(block, k)
        return remote(at, at, up_send.at[s, k], up_recv.at[s, k], (me + 2, g))

    def down_copy(block, k, s):
        at = piece(block, k)
        return remote(at, at, down_send.at[s, k], down_recv.at[s, k], (me - 2, g))

    def sib_copy(block, k, role):
        at = piece(block, k)
        return remote(at, at, sib_send.at[role, k], sib_recv.at[role, k], (sib, g))

    def across_copy():
        return remote(
            feats_ref, far_feats.at[0], far_send.at[0], far_recv.at[0], (across, g)
        )

    def far_copy(j):
        return remote(
            far_feats.at[0], far_feats.at[n_group - j], far_send.at[j],
            far_recv.at[n_group - j], (me, (g + j) % n_group),
        )

    def far_sib_copy(block, k):
        at = piece(block, k)
        return remote(at, at, far_sib_send.at[k], far_sib_recv.at[k], (sib, g))

    def far_share():
        across_copy().wait_recv()
        for j in range(1, n_group):
            far_copy(j).start()

    def far_project():
        for k in range(n_group):
            if k:
                far_copy(n_group - k).wait_recv()
            step = 256

            @pl.loop(0, rows // step)
            def _(i):
                at = pl.multiple_of(i * step, step)
                found = jnp.dot(
                    far_feats[k, pl.ds(at, step), :], w_ref[:, wide:],
                    preferred_element_type=jnp.float32,
                ).astype(jnp.bfloat16)
                for m in range(step // TILE):
                    tile = place(across, k) + i * (step // TILE) + m
                    kv_ref[tile] = found[m * TILE : (m + 1) * TILE]

            far_sib_copy(across, k).start()

    def far_finish():
        across_copy().wait_send()
        for j in range(1, n_group):
            far_copy(j).wait_send()
        for k in range(n_group):
            far_sib_copy(across, k).wait_send()
            far_sib_copy(across + 1 - 2 * core, k).wait_recv()

    for j in range(1, n_group):
        feat_copy(j).start()
    pl.when(at_end)(lambda: across_copy().start())

    def own_piece(k):
        if k:
            feat_copy(n_group - k).wait_recv()
        source = feats_ref if k == 0 else arrived.at[k - 1]
        base = pl.multiple_of(((g + k) % n_group) * rows, rows)
        step = 256

        @pl.loop(0, rows // step)
        def _(i):
            at = pl.multiple_of(i * step, step)
            both = jnp.dot(
                source[pl.ds(at, step), :], w_ref[...], preferred_element_type=jnp.float32
            ).astype(jnp.bfloat16)
            q_ref[pl.ds(pl.multiple_of(base + at, step), step), :] = both[:, :wide]
            for m in range(step // TILE):
                tile = place(me, k) + i * (step // TILE) + m
                kv_ref[tile] = both[m * TILE : (m + 1) * TILE, wide:]

        pl.when(has_up)(lambda: up_copy(me, k, 0).start())
        pl.when(has_down)(lambda: down_copy(me, k, 0).start())
        sib_copy(me, k, 0).start()

    def arrival(k, s):
        @pl.when(z - 1 - s >= 0)
        def _():
            block = me - 2 * (1 + s)
            up_copy(block, k, s).wait_recv()
            if s + 1 < chips - 2:
                pl.when(has_up)(lambda: up_copy(block, k, s + 1).start())
            sib_copy(block, k, 1 + s).start()

        @pl.when(z + 1 + s < chips)
        def _():
            block = me + 2 * (1 + s)
            down_copy(block, k, s).wait_recv()
            if s + 1 < chips - 2:
                pl.when(has_down)(lambda: down_copy(block, k, s + 1).start())
            sib_copy(block, k, chips + s).start()

    for t in range(n_group + chips - 2):
        if t < n_group:
            own_piece(t)
        if t == n_group - 1:
            for j in range(1, n_group):
                wout_copy(j, g).start()
            w_full_ref[pl.ds(pl.multiple_of(g * cut, cut), cut), :] = w_out_ref[...]
            pl.when(at_end)(far_share)
        for s in range(chips - 2):
            if 0 <= t - 1 - s < n_group:
                arrival(t - 1 - s, s)
        if t == n_group:
            pl.when(at_end)(far_project)

    for j in range(1, n_group):
        feat_copy(j).wait_send()
        wout_copy(j, g).wait_send()
        wout_copy(n_group - j, (g + j) % n_group).wait_recv()
    for k in range(n_group):
        sib_copy(me, k, 0).wait_send()
        sib_copy(sib, k, 0).wait_recv()
        for s in range(chips - 2):

            @pl.when(z - 1 - s >= 0)
            def _():
                sib_copy(me - 2 * (1 + s), k, 1 + s).wait_send()
                sib_copy(sib - 2 * (1 + s), k, 1 + s).wait_recv()

            @pl.when(z + 1 + s < chips)
            def _():
                sib_copy(me + 2 * (1 + s), k, chips + s).wait_send()
                sib_copy(sib + 2 * (1 + s), k, chips + s).wait_recv()

            @pl.when(has_up & (z - s >= 0))
            def _():
                up_copy(me - 2 * s, k, s).wait_send()

            @pl.when(has_down & (z + s < chips))
            def _():
                down_copy(me + 2 * s, k, s).wait_send()

    pl.when(at_end)(far_finish)

    def mix_copy(j, slot):
        return remote(
            mine.at[j - 1], landed.at[slot], mix_send.at[j - 1],
            mix_recv.at[n_group - j - 1], (me, (g + j) % n_group),
        )

    for j in [*range(1, n_group), 0]:
        first = ((g + j) % n_group) * (rows // TILE)

        @pl.loop(0, rows // TILE, unroll=2)
        def _(i):
            row = first + i
            at = pl.multiple_of(i * TILE, TILE)
            queries = q_ref[pl.ds(pl.multiple_of(row * TILE, TILE), TILE), :]
            mixed = attend_tile(cols_ref, row, queries, kv_ref, heads, head_dim)
            if j:
                mine[j - 1, pl.ds(at, TILE), :] = mixed
            else:
                landed[g, pl.ds(at, TILE), :] = mixed

        if j:
            mix_copy(j, g).start()

    for j in range(1, n_group):
        mix_copy(j, g).wait_send()
        mix_copy(n_group - j, (g + j) % n_group).wait_recv()

    @pl.loop(0, rows // 256)
    def _(i):
        at = pl.ds(pl.multiple_of(i * 256, 256), 256)
        mixed = jnp.concatenate([landed[m, at, :] for m in range(n_group)], axis=1)
        out_ref[at, :] = jnp.dot(
            mixed, w_full_ref[...], preferred_element_type=jnp.float32
        ).astype(out_ref.dtype)


def fused(cols, feats, weight, w_out, n_loop, n_group, heads, head_dim):
    rows, width = feats.shape
    wide = weight.shape[1] // 2
    chips = n_loop // 2
    vmem, dma = pl.BlockSpec(memory_space=pltpu.VMEM), pltpu.SemaphoreType.DMA
    return pl.pallas_call(
        functools.partial(fused_kernel, n_loop, n_group, heads, head_dim),
        in_specs=[pl.BlockSpec(memory_space=pltpu.SMEM), vmem, vmem, vmem],
        out_specs=vmem,
        out_shape=jax.ShapeDtypeStruct((rows, w_out.shape[1]), jnp.bfloat16),
        scratch_shapes=[
            pltpu.VMEM((n_loop * n_group * rows // TILE, TILE, wide), jnp.bfloat16),
            pltpu.VMEM((n_group * rows, wide), jnp.bfloat16),
            pltpu.VMEM((n_group * w_out.shape[0], w_out.shape[1]), jnp.bfloat16),
            pltpu.VMEM((n_group - 1, rows, width), jnp.bfloat16),
            dma((n_group - 1,)), dma((n_group - 1,)),
            dma((n_group - 1,)), dma((n_group - 1,)),
            dma((chips - 1, n_group)), dma((chips - 1, n_group)),
            dma((chips - 1, n_group)), dma((chips - 1, n_group)),
            dma((2 * chips - 1, n_group)), dma((2 * chips - 1, n_group)),
            pltpu.VMEM((n_group, rows, width), jnp.bfloat16),
            dma((n_group,)), dma((n_group,)), dma((n_group,)), dma((n_group,)),
            pltpu.VMEM((n_group - 1, rows, heads * head_dim), jnp.bfloat16),
            pltpu.VMEM((n_group, rows, heads * head_dim), jnp.bfloat16),
            dma((n_group - 1,)), dma((n_group - 1,)),
        ],
        compiler_params=pltpu.CompilerParams(
            collective_id=0, has_side_effects=True, vmem_limit_bytes=56 * 2**20
        ),
    )(cols, feats, weight, w_out)


def per_device(node_feats, w_qkv, w_out, tile_cols):
    width, heads, packed = w_qkv.shape
    head_dim = packed // 3
    n_loop, n_group = lax.axis_size("loop"), lax.axis_size("group")
    w_q = jnp.pad(w_qkv[:, :, :head_dim], ((0, 0), (0, 0), (0, head_dim)))
    w_q = w_q.reshape(width, heads * 2 * head_dim)
    w_kv = w_qkv[:, :, head_dim:].reshape(width, heads * 2 * head_dim)
    weight = jnp.concatenate([w_q, w_kv], axis=1)
    return fused(tile_cols, node_feats, weight, w_out, n_loop, n_group, heads, head_dim)


def solution(mesh):
    placed = (P(("loop", "group"), None), P(None, "group", None), P("group", None), P("loop", None))
    return jax.shard_map(
        per_device,
        mesh=mesh,
        in_specs=placed,
        out_specs=P(("loop", "group"), None),
        check_vma=False,
    )
```

```python
import functools

import jax
import jax.numpy as jnp
from jax import lax
from jax.experimental import pallas as pl
from jax.experimental.pallas import tpu as pltpu
from jax.sharding import PartitionSpec as P

TILE = 128
MESH = pl.DeviceIdType.MESH
LOG2E = 1.4426950408889634


def attend_tile(cols_ref, row, queries, kv_ref, heads, head_dim):
    slots = cols_ref.shape[1]
    wide = 2 * head_dim
    factor = LOG2E / head_dim**0.5
    tiles = [cols_ref[row, s] for s in range(slots)]
    mixed = []
    for h in range(heads):
        lanes = slice(h * wide, (h + 1) * wide)
        kv = jnp.concatenate([kv_ref[t, :, lanes] for t in tiles], axis=0)
        scores = lax.dot_general(
            queries[:, lanes], kv, (((1,), (1,)), ((), ())), preferred_element_type=jnp.float32
        )
        top = jnp.max(scores, axis=-1, keepdims=True)
        weights = jnp.exp2((scores - top) * factor)
        denom = jnp.sum(weights, axis=-1, keepdims=True)
        summed = jnp.dot(weights.astype(jnp.bfloat16), kv, preferred_element_type=jnp.float32)
        mixed.append((summed / denom)[:, head_dim:])
    return jnp.concatenate(mixed, axis=1).astype(jnp.bfloat16)


def fused_kernel(
    n_loop, n_group, heads, head_dim,
    cols_ref, feats_ref, w_ref, w_out_ref, out_ref, whole_ref, kv_ref, q_ref, w_full_ref, arrived,
    feat_send, feat_recv, wout_send, wout_recv, up_send, up_recv, down_send, down_recv,
    sib_send, sib_recv, far_feats, far_send, far_recv, far_sib_send, far_sib_recv,
    mine, landed, mix_send, mix_recv,
):
    me, g = lax.axis_index("loop"), lax.axis_index("group")
    core, z = me % 2, me // 2
    chips = n_loop // 2
    sib = me + 1 - 2 * core
    has_up, has_down = z < chips - 1, z > 0
    at_end = (z == 0) | (z == chips - 1)
    across = 2 * (chips - 1 - z) + core
    rows, wide = feats_ref.shape[0], kv_ref.shape[2]
    cut = w_out_ref.shape[0]

    barrier = pltpu.get_barrier_semaphore()

    def greet(device):
        pl.semaphore_signal(barrier, inc=1, device_id=device, device_id_type=MESH)

    for j in range(1, n_group):
        greet((me, (g + j) % n_group))
    greet((sib, g))
    pl.when(has_up)(lambda: greet((me + 2, g)))
    pl.when(has_down)(lambda: greet((me - 2, g)))
    pl.when(at_end)(lambda: greet((across, g)))
    greetings = n_group + jnp.where(at_end, 1, 0) + jnp.where(has_up, 1, 0) + jnp.where(has_down, 1, 0)
    pl.semaphore_wait(barrier, greetings)

    def remote(src, dst, send, recv, device):
        return pltpu.make_async_remote_copy(
            src_ref=src, dst_ref=dst, send_sem=send, recv_sem=recv,
            device_id=device, device_id_type=MESH,
        )

    def place(block, k):
        return (block * n_group + (g + k) % n_group) * (rows // TILE)

    def piece(block, k):
        return kv_ref.at[pl.ds(place(block, k), rows // TILE)]

    def feat_copy(j):
        return remote(
            feats_ref, arrived.at[n_group - j - 1], feat_send.at[j - 1],
            feat_recv.at[n_group - j - 1], (me, (g + j) % n_group),
        )

    def wout_copy(j, owner):
        part = w_full_ref.at[pl.ds(pl.multiple_of(owner * cut, cut), cut)]
        return remote(
            w_out_ref, part, wout_send.at[j - 1], wout_recv.at[n_group - j - 1],
            (me, (g + j) % n_group),
        )

    def up_copy(block, k, s):
        at = piece(block, k)
        return remote(at, at, up_send.at[s, k], up_recv.at[s, k], (me + 2, g))

    def down_copy(block, k, s):
        at = piece(block, k)
        return remote(at, at, down_send.at[s, k], down_recv.at[s, k], (me - 2, g))

    def sib_copy(block, k, role):
        at = piece(block, k)
        return remote(at, at, sib_send.at[role, k], sib_recv.at[role, k], (sib, g))

    def across_copy():
        return remote(
            feats_ref, far_feats.at[0], far_send.at[0], far_recv.at[0], (across, g)
        )

    def far_copy(j):
        return remote(
            far_feats.at[0], far_feats.at[n_group - j], far_send.at[j],
            far_recv.at[n_group - j], (me, (g + j) % n_group),
        )

    def far_sib_copy(block, k):
        at = piece(block, k)
        return remote(at, at, far_sib_send.at[k], far_sib_recv.at[k], (sib, g))

    def far_share():
        across_copy().wait_recv()
        for j in range(1, n_group):
            far_copy(j).start()

    def far_project():
        for k in range(n_group):
            if k:
                far_copy(n_group - k).wait_recv()
            step = 256

            @pl.loop(0, rows // step)
            def _(i):
                at = pl.multiple_of(i * step, step)
                found = jnp.dot(
                    far_feats[k, pl.ds(at, step), :], w_ref[:, wide:],
                    preferred_element_type=jnp.float32,
                ).astype(jnp.bfloat16)
                for m in range(step // TILE):
                    tile = place(across, k) + i * (step // TILE) + m
                    kv_ref[tile] = found[m * TILE : (m + 1) * TILE]

            far_sib_copy(across, k).start()

    def far_finish():
        across_copy().wait_send()
        for j in range(1, n_group):
            far_copy(j).wait_send()
        for k in range(n_group):
            far_sib_copy(across, k).wait_send()
            far_sib_copy(across + 1 - 2 * core, k).wait_recv()

    for j in range(1, n_group):
        feat_copy(j).start()
    pl.when(at_end)(lambda: across_copy().start())

    def own_piece(k):
        if k:
            feat_copy(n_group - k).wait_recv()
        source = feats_ref if k == 0 else arrived.at[k - 1]
        base = pl.multiple_of(((g + k) % n_group) * rows, rows)
        step = 256

        @pl.loop(0, rows // step)
        def _(i):
            at = pl.multiple_of(i * step, step)
            both = jnp.dot(
                source[pl.ds(at, step), :], w_ref[...], preferred_element_type=jnp.float32
            ).astype(jnp.bfloat16)
            q_ref[pl.ds(pl.multiple_of(base + at, step), step), :] = both[:, :wide]
            for m in range(step // TILE):
                tile = place(me, k) + i * (step // TILE) + m
                kv_ref[tile] = both[m * TILE : (m + 1) * TILE, wide:]

        pl.when(has_up)(lambda: up_copy(me, k, 0).start())
        pl.when(has_down)(lambda: down_copy(me, k, 0).start())
        sib_copy(me, k, 0).start()

    def arrival(k, s):
        @pl.when(z - 1 - s >= 0)
        def _():
            block = me - 2 * (1 + s)
            up_copy(block, k, s).wait_recv()
            if s + 1 < chips - 2:
                pl.when(has_up)(lambda: up_copy(block, k, s + 1).start())
            sib_copy(block, k, 1 + s).start()

        @pl.when(z + 1 + s < chips)
        def _():
            block = me + 2 * (1 + s)
            down_copy(block, k, s).wait_recv()
            if s + 1 < chips - 2:
                pl.when(has_down)(lambda: down_copy(block, k, s + 1).start())
            sib_copy(block, k, chips + s).start()

    for t in range(n_group + chips - 2):
        if t < n_group:
            own_piece(t)
        if t == n_group - 1:
            for j in range(1, n_group):
                wout_copy(j, g).start()
            w_full_ref[pl.ds(pl.multiple_of(g * cut, cut), cut), :] = w_out_ref[...]
            pl.when(at_end)(far_share)
        for s in range(chips - 2):
            if 0 <= t - 1 - s < n_group:
                arrival(t - 1 - s, s)
        if t == n_group:
            pl.when(at_end)(far_project)

    for j in range(1, n_group):
        feat_copy(j).wait_send()
        wout_copy(j, g).wait_send()
        wout_copy(n_group - j, (g + j) % n_group).wait_recv()
    for k in range(n_group):
        sib_copy(me, k, 0).wait_send()
        sib_copy(sib, k, 0).wait_recv()
        for s in range(chips - 2):

            @pl.when(z - 1 - s >= 0)
            def _():
                sib_copy(me - 2 * (1 + s), k, 1 + s).wait_send()
                sib_copy(sib - 2 * (1 + s), k, 1 + s).wait_recv()

            @pl.when(z + 1 + s < chips)
            def _():
                sib_copy(me + 2 * (1 + s), k, chips + s).wait_send()
                sib_copy(sib + 2 * (1 + s), k, chips + s).wait_recv()

            @pl.when(has_up & (z - s >= 0))
            def _():
                up_copy(me - 2 * s, k, s).wait_send()

            @pl.when(has_down & (z + s < chips))
            def _():
                down_copy(me + 2 * s, k, s).wait_send()

    pl.when(at_end)(far_finish)

    def mix_copy(j, slot):
        return remote(
            mine.at[j - 1], landed.at[slot], mix_send.at[j - 1],
            mix_recv.at[n_group - j - 1], (me, (g + j) % n_group),
        )

    for j in [*range(1, n_group), 0]:
        first = ((g + j) % n_group) * (rows // TILE)

        @pl.loop(0, rows // TILE, unroll=2)
        def _(i):
            row = first + i
            at = pl.multiple_of(i * TILE, TILE)
            queries = q_ref[pl.ds(pl.multiple_of(row * TILE, TILE), TILE), :]
            mixed = attend_tile(cols_ref, row, queries, kv_ref, heads, head_dim)
            if j:
                mine[j - 1, pl.ds(at, TILE), :] = mixed
            else:
                landed[g, pl.ds(at, TILE), :] = mixed

        if j:
            mix_copy(j, g).start()

    for j in range(1, n_group):
        mix_copy(j, g).wait_send()
        mix_copy(n_group - j, (g + j) % n_group).wait_recv()

    @pl.loop(0, rows // 256)
    def _(i):
        at = pl.ds(pl.multiple_of(i * 256, 256), 256)
        out_ref[at, :] = jnp.concatenate([landed[m, at, :] for m in range(n_group)], axis=1)

    @pl.loop(0, n_group)
    def _(i):
        at = pl.ds(pl.multiple_of(i * cut, cut), cut)
        whole_ref[at, :] = w_full_ref[at, :]


def fused(cols, feats, weight, w_out, n_loop, n_group, heads, head_dim):
    rows, width = feats.shape
    wide = weight.shape[1] // 2
    chips = n_loop // 2
    vmem, dma = pl.BlockSpec(memory_space=pltpu.VMEM), pltpu.SemaphoreType.DMA
    return pl.pallas_call(
        functools.partial(fused_kernel, n_loop, n_group, heads, head_dim),
        in_specs=[pl.BlockSpec(memory_space=pltpu.SMEM), vmem, vmem, vmem],
        out_specs=[vmem, vmem],
        out_shape=[
            jax.ShapeDtypeStruct((rows, n_group * heads * head_dim), jnp.bfloat16),
            jax.ShapeDtypeStruct((n_group * w_out.shape[0], w_out.shape[1]), jnp.bfloat16),
        ],
        scratch_shapes=[
            pltpu.VMEM((n_loop * n_group * rows // TILE, TILE, wide), jnp.bfloat16),
            pltpu.VMEM((n_group * rows, wide), jnp.bfloat16),
            pltpu.VMEM((n_group * w_out.shape[0], w_out.shape[1]), jnp.bfloat16),
            pltpu.VMEM((n_group - 1, rows, width), jnp.bfloat16),
            dma((n_group - 1,)), dma((n_group - 1,)),
            dma((n_group - 1,)), dma((n_group - 1,)),
            dma((chips - 1, n_group)), dma((chips - 1, n_group)),
            dma((chips - 1, n_group)), dma((chips - 1, n_group)),
            dma((2 * chips - 1, n_group)), dma((2 * chips - 1, n_group)),
            pltpu.VMEM((n_group, rows, width), jnp.bfloat16),
            dma((n_group,)), dma((n_group,)), dma((n_group,)), dma((n_group,)),
            pltpu.VMEM((n_group - 1, rows, heads * head_dim), jnp.bfloat16),
            pltpu.VMEM((n_group, rows, heads * head_dim), jnp.bfloat16),
            dma((n_group - 1,)), dma((n_group - 1,)),
        ],
        compiler_params=pltpu.CompilerParams(
            collective_id=0, has_side_effects=True, vmem_limit_bytes=56 * 2**20
        ),
    )(cols, feats, weight, w_out)


def per_device(node_feats, w_qkv, w_out, tile_cols):
    width, heads, packed = w_qkv.shape
    head_dim = packed // 3
    n_loop, n_group = lax.axis_size("loop"), lax.axis_size("group")
    w_q = jnp.pad(w_qkv[:, :, :head_dim], ((0, 0), (0, 0), (0, head_dim)))
    w_q = w_q.reshape(width, heads * 2 * head_dim)
    w_kv = w_qkv[:, :, head_dim:].reshape(width, heads * 2 * head_dim)
    weight = jnp.concatenate([w_q, w_kv], axis=1)
    mixed, w_full = fused(
        tile_cols, node_feats, weight, w_out, n_loop, n_group, heads, head_dim
    )
    return jnp.dot(mixed, w_full, preferred_element_type=jnp.float32).astype(jnp.bfloat16)


def solution(mesh):
    placed = (P(("loop", "group"), None), P(None, "group", None), P("group", None), P("loop", None))
    return jax.shard_map(
        per_device,
        mesh=mesh,
        in_specs=placed,
        out_specs=P(("loop", "group"), None),
        check_vma=False,
    )
```

```python
import functools

import jax
import jax.numpy as jnp
from jax import lax
from jax.experimental import pallas as pl
from jax.experimental.pallas import tpu as pltpu
from jax.sharding import PartitionSpec as P

TILE = 128
MESH = pl.DeviceIdType.MESH
LOG2E = 1.4426950408889634


def attend_tile(cols_ref, row, queries, kv_ref, heads, head_dim):
    slots = cols_ref.shape[1]
    wide = 2 * head_dim
    factor = LOG2E / head_dim**0.5
    tiles = [cols_ref[row, s] for s in range(slots)]
    mixed = []
    for h in range(heads):
        lanes = slice(h * wide, (h + 1) * wide)
        kv = jnp.concatenate([kv_ref[t, :, lanes] for t in tiles], axis=0)
        scores = lax.dot_general(
            queries[:, lanes], kv, (((1,), (1,)), ((), ())), preferred_element_type=jnp.float32
        )
        top = jnp.max(scores, axis=-1, keepdims=True)
        weights = jnp.exp2((scores - top) * factor)
        denom = jnp.sum(weights, axis=-1, keepdims=True)
        summed = jnp.dot(weights.astype(jnp.bfloat16), kv, preferred_element_type=jnp.float32)
        mixed.append((summed / denom)[:, head_dim:])
    return jnp.concatenate(mixed, axis=1).astype(jnp.bfloat16)


def fused_kernel(
    n_loop, n_group, heads, head_dim,
    cols_ref, feats_ref, w_ref, w_out_ref, out_ref, kv_ref, q_ref, w_full_ref, arrived,
    feat_send, feat_recv, wout_send, wout_recv, up_send, up_recv, down_send, down_recv,
    sib_send, sib_recv, far_feats, far_send, far_recv, far_sib_send, far_sib_recv,
    mine, landed, mix_send, mix_recv,
):
    me, g = lax.axis_index("loop"), lax.axis_index("group")
    core, z = me % 2, me // 2
    chips = n_loop // 2
    sib = me + 1 - 2 * core
    has_up, has_down = z < chips - 1, z > 0
    at_end = (z == 0) | (z == chips - 1)
    across = 2 * (chips - 1 - z) + core
    rows, wide = feats_ref.shape[0], kv_ref.shape[2]
    cut = w_out_ref.shape[0]

    barrier = pltpu.get_barrier_semaphore()

    def greet(device):
        pl.semaphore_signal(barrier, inc=1, device_id=device, device_id_type=MESH)

    for j in range(1, n_group):
        greet((me, (g + j) % n_group))
    greet((sib, g))
    pl.when(has_up)(lambda: greet((me + 2, g)))
    pl.when(has_down)(lambda: greet((me - 2, g)))
    pl.when(at_end)(lambda: greet((across, g)))
    greetings = n_group + jnp.where(at_end, 1, 0) + jnp.where(has_up, 1, 0) + jnp.where(has_down, 1, 0)
    pl.semaphore_wait(barrier, greetings)

    def remote(src, dst, send, recv, device):
        return pltpu.make_async_remote_copy(
            src_ref=src, dst_ref=dst, send_sem=send, recv_sem=recv,
            device_id=device, device_id_type=MESH,
        )

    def place(block, k):
        return (block * n_group + (g + k) % n_group) * (rows // TILE)

    def piece(block, k):
        return kv_ref.at[pl.ds(place(block, k), rows // TILE)]

    def feat_copy(j):
        return remote(
            feats_ref, arrived.at[n_group - j - 1], feat_send.at[j - 1],
            feat_recv.at[n_group - j - 1], (me, (g + j) % n_group),
        )

    def wout_copy(j, owner):
        part = w_full_ref.at[pl.ds(pl.multiple_of(owner * cut, cut), cut)]
        return remote(
            w_out_ref, part, wout_send.at[j - 1], wout_recv.at[n_group - j - 1],
            (me, (g + j) % n_group),
        )

    def up_copy(block, k, s):
        at = piece(block, k)
        return remote(at, at, up_send.at[s, k], up_recv.at[s, k], (me + 2, g))

    def down_copy(block, k, s):
        at = piece(block, k)
        return remote(at, at, down_send.at[s, k], down_recv.at[s, k], (me - 2, g))

    def sib_copy(block, k, role):
        at = piece(block, k)
        return remote(at, at, sib_send.at[role, k], sib_recv.at[role, k], (sib, g))

    def across_copy():
        return remote(
            feats_ref, far_feats.at[0], far_send.at[0], far_recv.at[0], (across, g)
        )

    def far_copy(j):
        return remote(
            far_feats.at[0], far_feats.at[n_group - j], far_send.at[j],
            far_recv.at[n_group - j], (me, (g + j) % n_group),
        )

    def far_sib_copy(block, k):
        at = piece(block, k)
        return remote(at, at, far_sib_send.at[k], far_sib_recv.at[k], (sib, g))

    def far_share():
        across_copy().wait_recv()
        for j in range(1, n_group):
            far_copy(j).start()

    def far_project():
        for k in range(n_group):
            if k:
                far_copy(n_group - k).wait_recv()
            step = 256

            @pl.loop(0, rows // step)
            def _(i):
                at = pl.multiple_of(i * step, step)
                found = jnp.dot(
                    far_feats[k, pl.ds(at, step), :], w_ref[:, wide:],
                    preferred_element_type=jnp.float32,
                ).astype(jnp.bfloat16)
                for m in range(step // TILE):
                    tile = place(across, k) + i * (step // TILE) + m
                    kv_ref[tile] = found[m * TILE : (m + 1) * TILE]

            far_sib_copy(across, k).start()

    def far_finish():
        across_copy().wait_send()
        for j in range(1, n_group):
            far_copy(j).wait_send()
        for k in range(n_group):
            far_sib_copy(across, k).wait_send()
            far_sib_copy(across + 1 - 2 * core, k).wait_recv()

    for j in range(1, n_group):
        feat_copy(j).start()
    pl.when(at_end)(lambda: across_copy().start())

    def own_piece(k):
        if k:
            feat_copy(n_group - k).wait_recv()
        source = feats_ref if k == 0 else arrived.at[k - 1]
        base = pl.multiple_of(((g + k) % n_group) * rows, rows)
        step = 256

        @pl.loop(0, rows // step)
        def _(i):
            at = pl.multiple_of(i * step, step)
            both = jnp.dot(
                source[pl.ds(at, step), :], w_ref[...], preferred_element_type=jnp.float32
            ).astype(jnp.bfloat16)
            q_ref[pl.ds(pl.multiple_of(base + at, step), step), :] = both[:, :wide]
            for m in range(step // TILE):
                tile = place(me, k) + i * (step // TILE) + m
                kv_ref[tile] = both[m * TILE : (m + 1) * TILE, wide:]

        pl.when(has_up)(lambda: up_copy(me, k, 0).start())
        pl.when(has_down)(lambda: down_copy(me, k, 0).start())
        sib_copy(me, k, 0).start()

    def arrival(k, s):
        @pl.when(z - 1 - s >= 0)
        def _():
            block = me - 2 * (1 + s)
            up_copy(block, k, s).wait_recv()
            if s + 1 < chips - 2:
                pl.when(has_up)(lambda: up_copy(block, k, s + 1).start())
            sib_copy(block, k, 1 + s).start()

        @pl.when(z + 1 + s < chips)
        def _():
            block = me + 2 * (1 + s)
            down_copy(block, k, s).wait_recv()
            if s + 1 < chips - 2:
                pl.when(has_down)(lambda: down_copy(block, k, s + 1).start())
            sib_copy(block, k, chips + s).start()

    for t in range(n_group + chips - 2):
        if t < n_group:
            own_piece(t)
        if t == n_group - 1:
            for j in range(1, n_group):
                wout_copy(j, g).start()
            w_full_ref[pl.ds(pl.multiple_of(g * cut, cut), cut), :] = w_out_ref[...]
            pl.when(at_end)(far_share)
        for s in range(chips - 2):
            if 0 <= t - 1 - s < n_group:
                arrival(t - 1 - s, s)
        if t == n_group:
            pl.when(at_end)(far_project)

    for j in range(1, n_group):
        feat_copy(j).wait_send()
        wout_copy(j, g).wait_send()
        wout_copy(n_group - j, (g + j) % n_group).wait_recv()
    for k in range(n_group):
        sib_copy(me, k, 0).wait_send()
        sib_copy(sib, k, 0).wait_recv()
        for s in range(chips - 2):

            @pl.when(z - 1 - s >= 0)
            def _():
                sib_copy(me - 2 * (1 + s), k, 1 + s).wait_send()
                sib_copy(sib - 2 * (1 + s), k, 1 + s).wait_recv()

            @pl.when(z + 1 + s < chips)
            def _():
                sib_copy(me + 2 * (1 + s), k, chips + s).wait_send()
                sib_copy(sib + 2 * (1 + s), k, chips + s).wait_recv()

            @pl.when(has_up & (z - s >= 0))
            def _():
                up_copy(me - 2 * s, k, s).wait_send()

            @pl.when(has_down & (z + s < chips))
            def _():
                down_copy(me + 2 * s, k, s).wait_send()

    pl.when(at_end)(far_finish)

    def mix_copy(j, slot):
        return remote(
            mine.at[j - 1], landed.at[slot], mix_send.at[j - 1],
            mix_recv.at[n_group - j - 1], (me, (g + j) % n_group),
        )

    for j in [*range(1, n_group), 0]:
        first = ((g + j) % n_group) * (rows // TILE)

        @pl.loop(0, rows // TILE, unroll=4)
        def _(i):
            row = first + i
            at = pl.multiple_of(i * TILE, TILE)
            queries = q_ref[pl.ds(pl.multiple_of(row * TILE, TILE), TILE), :]
            mixed = attend_tile(cols_ref, row, queries, kv_ref, heads, head_dim)
            if j:
                mine[j - 1, pl.ds(at, TILE), :] = mixed
            else:
                landed[g, pl.ds(at, TILE), :] = mixed

        if j:
            mix_copy(j, g).start()

    for j in range(1, n_group):
        mix_copy(j, g).wait_send()
        mix_copy(n_group - j, (g + j) % n_group).wait_recv()

    @pl.loop(0, rows // 256)
    def _(i):
        at = pl.ds(pl.multiple_of(i * 256, 256), 256)
        mixed = jnp.concatenate([landed[m, at, :] for m in range(n_group)], axis=1)
        out_ref[at, :] = jnp.dot(
            mixed, w_full_ref[...], preferred_element_type=jnp.float32
        ).astype(out_ref.dtype)


def fused(cols, feats, weight, w_out, n_loop, n_group, heads, head_dim):
    rows, width = feats.shape
    wide = weight.shape[1] // 2
    chips = n_loop // 2
    vmem, dma = pl.BlockSpec(memory_space=pltpu.VMEM), pltpu.SemaphoreType.DMA
    return pl.pallas_call(
        functools.partial(fused_kernel, n_loop, n_group, heads, head_dim),
        in_specs=[pl.BlockSpec(memory_space=pltpu.SMEM), vmem, vmem, vmem],
        out_specs=vmem,
        out_shape=jax.ShapeDtypeStruct((rows, w_out.shape[1]), jnp.bfloat16),
        scratch_shapes=[
            pltpu.VMEM((n_loop * n_group * rows // TILE, TILE, wide), jnp.bfloat16),
            pltpu.VMEM((n_group * rows, wide), jnp.bfloat16),
            pltpu.VMEM((n_group * w_out.shape[0], w_out.shape[1]), jnp.bfloat16),
            pltpu.VMEM((n_group - 1, rows, width), jnp.bfloat16),
            dma((n_group - 1,)), dma((n_group - 1,)),
            dma((n_group - 1,)), dma((n_group - 1,)),
            dma((chips - 1, n_group)), dma((chips - 1, n_group)),
            dma((chips - 1, n_group)), dma((chips - 1, n_group)),
            dma((2 * chips - 1, n_group)), dma((2 * chips - 1, n_group)),
            pltpu.VMEM((n_group, rows, width), jnp.bfloat16),
            dma((n_group,)), dma((n_group,)), dma((n_group,)), dma((n_group,)),
            pltpu.VMEM((n_group - 1, rows, heads * head_dim), jnp.bfloat16),
            pltpu.VMEM((n_group, rows, heads * head_dim), jnp.bfloat16),
            dma((n_group - 1,)), dma((n_group - 1,)),
        ],
        compiler_params=pltpu.CompilerParams(
            collective_id=0, has_side_effects=True, vmem_limit_bytes=56 * 2**20
        ),
    )(cols, feats, weight, w_out)


def per_device(node_feats, w_qkv, w_out, tile_cols):
    width, heads, packed = w_qkv.shape
    head_dim = packed // 3
    n_loop, n_group = lax.axis_size("loop"), lax.axis_size("group")
    w_q = jnp.pad(w_qkv[:, :, :head_dim], ((0, 0), (0, 0), (0, head_dim)))
    w_q = w_q.reshape(width, heads * 2 * head_dim)
    w_kv = w_qkv[:, :, head_dim:].reshape(width, heads * 2 * head_dim)
    weight = jnp.concatenate([w_q, w_kv], axis=1)
    return fused(tile_cols, node_feats, weight, w_out, n_loop, n_group, heads, head_dim)


def solution(mesh):
    placed = (P(("loop", "group"), None), P(None, "group", None), P("group", None), P("loop", None))
    return jax.shard_map(
        per_device,
        mesh=mesh,
        in_specs=placed,
        out_specs=P(("loop", "group"), None),
        check_vma=False,
    )
```
